128 devices in a mesh: band: 16 (over z, y_lo, core), blk: 8 (over x, y_hi).
Axes of the slice: x: 4, y: 4 (y_hi: 2, y_lo: 2; y = y_hi * 2 + y_lo), z: 4, core: 2. Of those that a mesh axis runs over, the one named last changes fastest.
Arguments:
- steering: bfloat16 [8, 12288, 512], P('blk', 'band'), may hold values from -1.4 to 1.4
- estimates: bfloat16 [8, 12288], P('blk', 'band'), may hold values from 0 to 1
- spectra: float32 [8, 256, 512], P('blk', 'band'), may hold values from -768 to 8151
Outputs:
- updated: float32 [8, 12288], P('blk', 'band')
- broadband: float32 [12288], P('band')
The draws below stay inside these ranges and needn't reach their ends.
All inputs are finite; a program needn't handle non-finite values.
Results may differ from the reference program's by a relative error of at most 0.0003.
Values may be sent and summed in bfloat16 or wider, within the bound.
No kernel may reach another device: no remote copies, remote signals or barrier semaphores. Data moves between devices by JAX's collectives and lax.ppermute only.
A program may use at most 192 MiB of HBM per device.

```python
import math
import jax
import jax.numpy as jnp
from jax import lax

CHANNELS = 256
GRID_DEV = 768
GRID = 12288
BANDS = 8


def draw_steering(key, part):
    phase_key = jax.random.fold_in(key, 11)
    level_key = jax.random.fold_in(key, 12)
    shape = (BANDS, GRID, CHANNELS)
    phase = jax.random.uniform(phase_key, shape, jnp.float32, -math.pi, math.pi)
    amplitude = jnp.exp(jax.random.uniform(level_key, shape, jnp.float32, math.log(0.7), math.log(1.4)))
    result = jnp.concatenate([amplitude * jnp.cos(phase), amplitude * jnp.sin(phase)], axis=2)
    return result.astype(jnp.bfloat16)


def draw_spectra(key, part):
    noise_key = jax.random.fold_in(key, 21)
    level_key = jax.random.fold_in(key, 22)
    shape = (BANDS, CHANNELS, 2 * CHANNELS)
    noise = jnp.clip(jax.random.normal(noise_key, shape, jnp.float32), -3.0, 3.0)
    noise = noise * CHANNELS
    rows = lax.broadcasted_iota(jnp.int32, (CHANNELS, 2 * CHANNELS), 0)
    columns = lax.broadcasted_iota(jnp.int32, (CHANNELS, 2 * CHANNELS), 1)
    band_keys = jax.random.split(level_key, BANDS)
    order = jax.vmap(lambda one_key: jax.random.permutation(one_key, CHANNELS))(band_keys)
    fraction = order.astype(jnp.float32) * 4.0 / (CHANNELS - 1)
    level = ((9.0 + fraction) * ((CHANNELS + GRID) // 20)).reshape(BANDS, CHANNELS, 1)
    result = jnp.where(rows == columns, level, jnp.where(columns == rows + CHANNELS, 0.0, noise))
    return result.astype(jnp.float32)


def block_levels(own_key, extent, pieces, least, largest):
    level, own = 1.0, jax.random.fold_in(own_key, 6)
    for position, parts in pieces:
        heights = jnp.exp(jax.random.uniform(jax.random.fold_in(own, position), (parts,), jnp.float32, least / len(pieces), largest / len(pieces)))
        level = level * jnp.repeat(heights, extent[position] // parts).reshape([-1 if axis == position else 1 for axis in range(len(extent))])
    return level


def setup_inputs(seed: int = 0) -> dict:
    keys = jax.random.split(jax.random.key(seed), 4)
    steering = draw_steering(jax.random.fold_in(keys[3], 71), 0)
    estimates = jnp.clip(1.0 * jax.random.uniform(keys[1], (BANDS, GRID), jnp.float32) ** block_levels(keys[1], (BANDS, GRID), ((0, 8), (1, 16)), -0.2, 0.2), 0.0, 1.0).astype(jnp.bfloat16)
    spectra = draw_spectra(jax.random.fold_in(keys[3], 71), 0)
    return {"steering": steering, "estimates": estimates, "spectra": spectra}


def beam_map(steer_wide, cross):
    width = CHANNELS
    cross_real = cross[:, :width]
    cross_imag = cross[:, width:]
    kernel_real = jnp.concatenate([cross_real, -cross_imag], axis=1)
    kernel_imag = jnp.concatenate([cross_imag, cross_real], axis=1)
    real_part = jnp.dot(steer_wide, kernel_real.T, precision=lax.Precision.HIGHEST, preferred_element_type=jnp.float32)
    imag_part = jnp.dot(steer_wide, kernel_imag.T, precision=lax.Precision.HIGHEST, preferred_element_type=jnp.float32)
    summed = jnp.sum(steer_wide[:, :width] * real_part + steer_wide[:, width:] * imag_part, axis=1)
    return summed / (width * width)


def band_update(operands):
    steering, estimates, spectra = operands
    width = CHANNELS
    steer_wide = steering.astype(jnp.float32)
    beam = beam_map(steer_wide, spectra)
    turned = jnp.concatenate([-steering[:, width:], steering[:, :width]], axis=1)
    values = estimates.astype(jnp.float32)
    blocks = steering.reshape(GRID // GRID_DEV, GRID_DEV, 2 * width)
    turned_blocks = turned.reshape(GRID // GRID_DEV, GRID_DEV, 2 * width)

    def one_block(pair):
        rows, turned_rows = pair
        real_sum = jnp.dot(rows, steering.T, preferred_element_type=jnp.float32)
        imag_sum = jnp.dot(turned_rows, steering.T, preferred_element_type=jnp.float32)
        tile = (real_sum * real_sum + imag_sum * imag_sum) / (width * width)
        return jnp.dot(tile, values, precision=lax.Precision.HIGHEST, preferred_element_type=jnp.float32)

    applied = lax.map(one_block, (blocks, turned_blocks)).reshape(GRID)
    power = jnp.sum(steer_wide * steer_wide, axis=1)
    diag = power * power / (width * width)
    return jnp.maximum(values + (beam - applied) / diag, 0.0)


def reference(steering, estimates, spectra):
    updated = lax.map(band_update, (steering, estimates, spectra))
    return updated, jnp.sum(updated, axis=0)
```

```python
import jax
import jax.numpy as jnp
from jax import lax
from jax.sharding import PartitionSpec as P

CHANNELS = 256


def exchange(value, axis, size, bit):
    return lax.ppermute(value, axis, [(i, i ^ bit) for i in range(size)])


def split_dot(exact, wide, contract):
    high = lax.reduce_precision(wide, 8, 7)
    low = (wide - high).astype(jnp.bfloat16)
    high = high.astype(jnp.bfloat16)
    dims = ((contract, (0,)), ((), ()))
    total = lax.dot_general(exact, high, dims, preferred_element_type=jnp.float32)
    return total + lax.dot_general(exact, low, dims, preferred_element_type=jnp.float32)


def body(steering, estimates, spectra):
    width = CHANNELS
    steering, spectra = steering[0], spectra[0]
    count = spectra.shape[0]
    index = lax.axis_index("band")
    core = lax.rem(index, 2)
    real, imag = steering[:, :width], steering[:, width:]
    real_wide, imag_wide = real.astype(jnp.float32), imag.astype(jnp.float32)
    values = estimates[0].astype(jnp.float32)
    minus, plus = real_wide - imag_wide, real_wide + imag_wide
    both = jnp.concatenate([real, imag], axis=0)
    mixed = jnp.concatenate([minus, plus], axis=0)
    twice = jnp.concatenate([values, values])[:, None]
    own = split_dot(both, mixed * twice, (0,))
    rows = (spectra[:, :width] + spectra[:, width:]) * 0.5
    columns = (spectra[:, :width] - spectra[:, width:]) * 0.5
    empty = jnp.zeros((width, width), jnp.float32)
    start = index * count
    placed = lax.dynamic_update_slice(empty, rows, (start, 0))
    turned = lax.dynamic_update_slice(empty, columns, (start, 0)).T
    packed = placed + turned - own
    half = width // 2
    send = lax.dynamic_slice_in_dim(packed, (1 - core) * half, half, 0)
    keep = lax.dynamic_slice_in_dim(packed, core * half, half, 0)
    keep = keep + exchange(send, "band", 16, 1)
    for bit in (2, 4, 8):
        keep = keep + exchange(keep, "band", 16, bit)
    other = exchange(keep, "band", 16, 1)
    low_half = jnp.where(core == 0, keep, other)
    high_half = jnp.where(core == 0, other, keep)
    packed = jnp.concatenate([low_half, high_half], axis=0)
    form = jnp.sum(split_dot(both, packed, (1,)) * mixed, axis=1)
    form = form[: values.shape[0]] + form[values.shape[0] :]
    scale = 1.0 / (width * width)
    power = jnp.sum(real_wide * real_wide + imag_wide * imag_wide, axis=1)
    diag = power * power * scale
    updated = jnp.maximum(values + form * scale / diag, 0.0)
    total = updated
    for bit in (1, 2, 4):
        total = total + exchange(total, "blk", 8, bit)
    return updated[None], total


def solution(mesh):
    return jax.shard_map(
        body,
        mesh=mesh,
        in_specs=(P("blk", "band", None), P("blk", "band"), P("blk", "band", None)),
        out_specs=(P("blk", "band"), P("band")),
        check_vma=False,
    )
```

```python
import functools

import jax
import jax.numpy as jnp
from jax import lax
from jax.experimental import pallas as pl
from jax.experimental.pallas import tpu as pltpu
from jax.sharding import PartitionSpec as P

CHANNELS = 256
HALF = CHANNELS // 2
CHUNK = 256
ORDER = ((0, 1, 3), (1, 3, 0))
VMEM = pl.BlockSpec(memory_space=pltpu.VMEM)
ANY = pl.BlockSpec(memory_space=pl.ANY)


def wide(*shape):
    return jax.ShapeDtypeStruct(shape, jnp.float32)


def call(kernel, out_shape, operands, scratch=(), flops=1 << 28, spec=VMEM, room=24):
    return pl.pallas_call(
        kernel,
        out_shape=out_shape,
        in_specs=[spec] * len(operands),
        out_specs=jax.tree.map(lambda _: VMEM, out_shape),
        scratch_shapes=list(scratch),
        compiler_params=pltpu.CompilerParams(vmem_limit_bytes=room << 20),
        cost_estimate=pl.CostEstimate(flops=flops, bytes_accessed=1 << 20, transcendentals=0),
    )(*operands)


def parts(value):
    high = value.astype(jnp.bfloat16)
    low = (value - high.astype(jnp.float32)).astype(jnp.bfloat16)
    return jnp.concatenate([high, low], axis=0)


def dot(left, right, contract):
    dims = (((1,), (contract,)), ((), ()))
    return lax.dot_general(left, right, dims, preferred_element_type=jnp.float32)


def folded(both):
    rows = both.shape[0] // 2
    return both[:rows] + both[rows:]


def place(index):
    return lax.rem(index + lax.div(index, 2) + lax.div(index, 4), 2)


def products(steering, values, first, rows):
    real = steering[rows, pl.ds(first, HALF)].T.astype(jnp.float32)
    imag = steering[rows, pl.ds(CHANNELS + first, HALF)].T.astype(jnp.float32)
    total = dot(parts((real - imag) * values), steering[rows, :CHANNELS], 0)
    return total + dot(parts((real + imag) * values), steering[rows, CHANNELS:], 0)


def cross_half(spectra, placed, half, own, out):
    count = spectra.shape[0]
    first = pl.multiple_of(half * HALF, HALF)
    row = pl.multiple_of(lax.axis_index("band") * count, count)
    cross_real, cross_imag = spectra[:, :CHANNELS], spectra[:, CHANNELS:]
    placed[...] = jnp.zeros_like(placed)
    placed[pl.ds(row, count), :] = (cross_real + cross_imag) * 0.5
    out[...] = placed[:, pl.ds(first, HALF)].T - own

    @pl.when(lax.div(row, HALF) == half)
    def _():
        here = pl.ds(pl.multiple_of(row - first, count), count)
        out[here, :] = out[here, :] + (cross_real - cross_imag) * 0.5


def first_kernel(steering_far, estimates_far, spectra_far, out, steering, estimates, spectra, placed, sems):
    starts = range(0, steering.shape[0], CHUNK)
    loads = [
        pltpu.make_async_copy(estimates_far, estimates, sems.at[0]),
        pltpu.make_async_copy(spectra_far, spectra, sems.at[1]),
    ]
    chunks = [
        pltpu.make_async_copy(steering_far.at[pl.ds(s, CHUNK)], steering.at[pl.ds(s, CHUNK)], sems.at[2 + n])
        for n, s in enumerate(starts)
    ]
    loads[0].start()
    for chunk in chunks:
        chunk.start()
    loads[1].start()
    half = 1 - place(lax.axis_index("band"))
    first = pl.multiple_of(half * HALF, HALF)
    loads[0].wait()
    own = jnp.zeros((2 * HALF, CHANNELS), jnp.float32)
    for s, chunk in zip(starts, chunks):
        chunk.wait()
        values = estimates[:, s : s + CHUNK].astype(jnp.float32)
        own = own + products(steering, values, first, slice(s, s + CHUNK))
    loads[1].wait()
    cross_half(spectra, placed, half, folded(own), out)


def second_kernel(steering, estimates, spectra, out, placed):
    half = place(lax.axis_index("band"))
    values = estimates[...].astype(jnp.float32)
    own = products(steering, values, pl.multiple_of(half * HALF, HALF), slice(None))
    cross_half(spectra, placed, half, folded(own), out)


def ready_kernel(steering, minus, plus, power):
    real = steering[:, :CHANNELS].T.astype(jnp.float32)
    imag = steering[:, CHANNELS:].T.astype(jnp.float32)
    minus[...] = real - imag
    plus[...] = real + imag
    power[...] = jnp.sum(real * real + imag * imag, axis=0, keepdims=True)


def form_kernel(mine, other, steering, estimates, minus, plus, power, updated, again, packed):
    half = place(lax.axis_index("band"))
    packed[pl.ds(pl.multiple_of(half * HALF, HALF), HALF), :] = mine[...]
    packed[pl.ds(pl.multiple_of((1 - half) * HALF, HALF), HALF), :] = other[...]
    pieces = parts(packed[...])
    scale = 1.0 / (CHANNELS * CHANNELS)
    for s in range(0, steering.shape[0], CHUNK):
        here = slice(s, s + CHUNK)
        form = folded(dot(pieces, steering[here, :CHANNELS], 1)) * minus[:, here]
        form = form + folded(dot(pieces, steering[here, CHANNELS:], 1)) * plus[:, here]
        form = jnp.sum(form, axis=0, keepdims=True)
        diag = power[:, here] * power[:, here] * scale
        result = jnp.maximum(estimates[:, here].astype(jnp.float32) + form * scale / diag, 0.0)
        updated[:, here] = result
        again[:, here] = result


def partner(index, step):
    z, y, core = index // 4, index // 2 % 2, index % 2
    kind = ORDER[(z + y + core) % 2][step]
    z, y = (z, 1 - y) if kind == 0 else (z ^ kind, y)
    return (z * 2 + y) * 2 + 1 - core


def body(steering, estimates, spectra):
    points = steering.shape[1]
    steering, spectra = steering[0], spectra[0]
    scratch = [pltpu.VMEM((CHANNELS, CHANNELS), jnp.float32)]
    count = points // CHUNK
    send, steering, estimates, spectra = call(
        first_kernel,
        (wide(HALF, CHANNELS), *(jax.ShapeDtypeStruct(a.shape, a.dtype) for a in (steering, estimates, spectra))),
        tuple(pltpu.with_memory_space_constraint(a, pltpu.HBM) for a in (steering, estimates, spectra)),
        scratch + [pltpu.SemaphoreType.DMA((2 + count,))],
        spec=ANY,
        room=24,
    )
    keep = call(second_kernel, wide(HALF, CHANNELS), (steering, estimates, spectra), scratch)
    twins = [(i, i ^ 1) for i in range(16)]
    total = keep + lax.ppermute(send, "band", twins)
    later, total = lax.optimization_barrier((steering, total))
    flat = wide(CHANNELS, points)
    ready = call(ready_kernel, (flat, flat, wide(1, points)), (later,))
    for step in range(3):
        total = total + lax.ppermute(total, "band", [(i, partner(i, step)) for i in range(16)])
        if step == 0:
            total, ready = lax.optimization_barrier((total, ready))
    other = lax.ppermute(total, "band", twins)
    updated, broadband = call(
        form_kernel, (wide(1, points),) * 2, (total, other, steering, estimates, *ready), scratch
    )

    def across(value, bit):
        return lax.ppermute(value, "blk", [(i, i ^ bit) for i in range(8)])

    for bit in (1, 2, 6):
        broadband = broadband + across(broadband, bit)
    return updated, broadband[0]


def solution(mesh):
    return jax.shard_map(
        body,
        mesh=mesh,
        in_specs=(P("blk", "band", None), P("blk", "band"), P("blk", "band", None)),
        out_specs=(P("blk", "band"), P("band")),
        check_vma=False,
    )
```

```python
import functools

import jax
import jax.numpy as jnp
from jax import lax
from jax.experimental import pallas as pl
from jax.experimental.pallas import tpu as pltpu
from jax.sharding import PartitionSpec as P

CHANNELS = 256
HALF = CHANNELS // 2
CHUNK = 256
FIRST = 768
LANES = 128
ORDER = ((0, 3, 1), (3, 1, 0))
VMEM = pl.BlockSpec(memory_space=pltpu.VMEM)
ANY = pl.BlockSpec(memory_space=pl.ANY)


def wide(*shape):
    return jax.ShapeDtypeStruct(shape, jnp.float32)


def call(kernel, out_shape, operands, scratch=(), flops=1 << 28, spec=VMEM, room=24):
    return pl.pallas_call(
        kernel,
        out_shape=out_shape,
        in_specs=[spec] * len(operands),
        out_specs=jax.tree.map(lambda _: VMEM, out_shape),
        scratch_shapes=list(scratch),
        compiler_params=pltpu.CompilerParams(vmem_limit_bytes=room << 20),
        cost_estimate=pl.CostEstimate(flops=flops, bytes_accessed=1 << 20, transcendentals=0),
    )(*operands)


def parts(value):
    high = value.astype(jnp.bfloat16)
    low = (value - high.astype(jnp.float32)).astype(jnp.bfloat16)
    return jnp.concatenate([high, low], axis=0)


def dot(left, right, contract):
    dims = (((1,), (contract,)), ((), ()))
    return lax.dot_general(left, right, dims, preferred_element_type=jnp.float32)


def folded(both):
    rows = both.shape[0] // 2
    return both[:rows] + both[rows:]


def place(index):
    return lax.rem(index + lax.div(index, 2) + lax.div(index, 4), 2)


def products(steering, values, first, rows):
    real = steering[rows, pl.ds(first, HALF)].T.astype(jnp.float32)
    imag = steering[rows, pl.ds(CHANNELS + first, HALF)].T.astype(jnp.float32)
    total = dot(parts((real - imag) * values), steering[rows, :CHANNELS], 0)
    return total + dot(parts((real + imag) * values), steering[rows, CHANNELS:], 0)


def cross_half(spectra, placed, half, out):
    count = spectra.shape[0]
    first = pl.multiple_of(half * HALF, HALF)
    row = pl.multiple_of(lax.axis_index("band") * count, count)
    cross_real, cross_imag = spectra[:, :CHANNELS], spectra[:, CHANNELS:]
    placed[...] = jnp.zeros_like(placed)
    placed[pl.ds(row, count), :] = (cross_real + cross_imag) * 0.5
    out[...] = placed[:, pl.ds(first, HALF)].T

    @pl.when(lax.div(row, HALF) == half)
    def _():
        here = pl.ds(pl.multiple_of(row - first, count), count)
        out[here, :] = out[here, :] + (cross_real - cross_imag) * 0.5


def first_kernel(steering_far, estimates_far, spectra_far, out, steering, estimates, spectra, placed, sems):
    starts = range(0, steering.shape[0], FIRST)
    loads = [
        pltpu.make_async_copy(estimates_far, estimates, sems.at[0]),
        pltpu.make_async_copy(spectra_far, spectra, sems.at[1]),
    ]
    chunks = [
        pltpu.make_async_copy(steering_far.at[pl.ds(s, FIRST)], steering.at[pl.ds(s, FIRST)], sems.at[2 + n])
        for n, s in enumerate(starts)
    ]
    for load in loads + chunks:
        load.start()
    half = 1 - place(lax.axis_index("band"))
    first = pl.multiple_of(half * HALF, HALF)
    loads[1].wait()
    cross_half(spectra, placed, half, out)
    loads[0].wait()
    own = jnp.zeros((2 * HALF, CHANNELS), jnp.float32)
    for s, chunk in zip(starts, chunks):
        chunk.wait()
        values = estimates[:, s : s + FIRST].astype(jnp.float32)
        own = own + products(steering, values, first, slice(s, s + FIRST))
    out[...] = out[...] - folded(own)


def second_kernel(steering, estimates, spectra, out, placed):
    half = place(lax.axis_index("band"))
    values = estimates[...].astype(jnp.float32)
    own = products(steering, values, pl.multiple_of(half * HALF, HALF), slice(None))
    cross_half(spectra, placed, half, out)
    out[...] = out[...] - folded(own)


def ready_kernel(steering, minus, plus, power):
    real = steering[:, :CHANNELS].T.astype(jnp.float32)
    imag = steering[:, CHANNELS:].T.astype(jnp.float32)
    minus[...] = real - imag
    plus[...] = real + imag
    power[...] = jnp.sum(real * real + imag * imag, axis=0, keepdims=True)


def form(total, half, steering, minus, plus, here):
    pieces = parts(total)
    rows = pl.ds(pl.multiple_of(half * HALF, HALF), HALF)
    terms = folded(dot(pieces, steering[here, :CHANNELS], 1)) * minus[rows, here]
    terms = terms + folded(dot(pieces, steering[here, CHANNELS:], 1)) * plus[rows, here]
    return jnp.sum(terms, axis=0, keepdims=True)


def near_kernel(mine, steering, minus, plus, partial):
    half = place(lax.axis_index("band"))
    for s in range(0, steering.shape[0], CHUNK):
        here = slice(s, s + CHUNK)
        partial[:, here] = form(mine[...], half, steering, minus, plus, here)


def far_kernel(other, partial, steering, estimates, minus, plus, power, updated):
    half = 1 - place(lax.axis_index("band"))
    scale = 1.0 / (CHANNELS * CHANNELS)
    for s in range(0, steering.shape[0], CHUNK):
        here = slice(s, s + CHUNK)
        whole = partial[:, here] + form(other[...], half, steering, minus, plus, here)
        diag = power[:, here] * power[:, here] * scale
        result = jnp.maximum(estimates[:, here].astype(jnp.float32) + whole * scale / diag, 0.0)
        for t in range(0, CHUNK, LANES):
            line = (s + t) // LANES
            updated[line : line + 1, :] = result[:, t : t + LANES]


def partner(index, step):
    z, y, core = index // 4, index // 2 % 2, index % 2
    kind = ORDER[(z + y + core) % 2][step]
    z, y = (z, 1 - y) if kind == 0 else (z ^ kind, y)
    return (z * 2 + y) * 2 + 1 - core


def body(steering, estimates, spectra):
    points = steering.shape[1]
    steering, spectra = steering[0], spectra[0]
    scratch = [pltpu.VMEM((CHANNELS, CHANNELS), jnp.float32)]
    count = points // FIRST
    send, steering, estimates, spectra = call(
        first_kernel,
        (wide(HALF, CHANNELS), *(jax.ShapeDtypeStruct(a.shape, a.dtype) for a in (steering, estimates, spectra))),
        tuple(pltpu.with_memory_space_constraint(a, pltpu.HBM) for a in (steering, estimates, spectra)),
        scratch + [pltpu.SemaphoreType.DMA((2 + count,))],
        spec=ANY,
        room=24,
    )
    keep = call(second_kernel, wide(HALF, CHANNELS), (steering, estimates, spectra), scratch)
    twins = [(i, i ^ 1) for i in range(16)]
    total = keep + lax.ppermute(send, "band", twins)
    later, total = lax.optimization_barrier((steering, total))
    flat = wide(CHANNELS, points)
    ready = call(ready_kernel, (flat, flat, wide(1, points)), (later,))
    for step in range(3):
        total = total + lax.ppermute(total, "band", [(i, partner(i, step)) for i in range(16)])
        if step == 0:
            total, ready = lax.optimization_barrier((total, ready))
    other = lax.ppermute(total, "band", twins)
    partial = call(near_kernel, wide(1, points), (total, steering, *ready[:2]))
    updated = call(far_kernel, wide(points // LANES, LANES), (other, partial, steering, estimates, *ready))
    broadband = updated

    def across(value, bit):
        return lax.ppermute(value, "blk", [(i, i ^ bit) for i in range(8)])

    for bit in (1, 2, 6):
        broadband = broadband + across(broadband, bit)
    return updated.reshape(1, points), broadband.reshape(points)


def solution(mesh):
    return jax.shard_map(
        body,
        mesh=mesh,
        in_specs=(P("blk", "band", None), P("blk", "band"), P("blk", "band", None)),
        out_specs=(P("blk", "band"), P("band")),
        check_vma=False,
    )
```

```python
import functools

import jax
import jax.numpy as jnp
from jax import lax
from jax.experimental import pallas as pl
from jax.experimental.pallas import tpu as pltpu
from jax.sharding import PartitionSpec as P

CHANNELS = 256
HALF = CHANNELS // 2
CHUNK = 256
FIRST = 768
LANES = 128
TAIL = 16
FLIPPED = (1, 2)
SUBLANES = 8
ORDER = ((0, 3, 1), (3, 1, 0))
VMEM = pl.BlockSpec(memory_space=pltpu.VMEM)
ANY = pl.BlockSpec(memory_space=pl.ANY)


def wide(*shape):
    return jax.ShapeDtypeStruct(shape, jnp.float32)


def call(kernel, out_shape, operands, scratch=(), flops=1 << 28, spec=VMEM, room=24):
    return pl.pallas_call(
        kernel,
        out_shape=out_shape,
        in_specs=[spec] * len(operands),
        out_specs=jax.tree.map(lambda _: VMEM, out_shape),
        scratch_shapes=list(scratch),
        compiler_params=pltpu.CompilerParams(vmem_limit_bytes=room << 20),
        cost_estimate=pl.CostEstimate(flops=flops, bytes_accessed=1 << 20, transcendentals=0),
    )(*operands)


def parts(value):
    high = value.astype(jnp.bfloat16)
    low = (value - high.astype(jnp.float32)).astype(jnp.bfloat16)
    return jnp.concatenate([high, low], axis=0)


def dot(left, right, contract):
    dims = (((1,), (contract,)), ((), ()))
    return lax.dot_general(left, right, dims, preferred_element_type=jnp.float32)


def folded(both):
    rows = both.shape[0] // 2
    return both[:rows] + both[rows:]


def place(index):
    return lax.rem(index + lax.div(index, 2) + lax.div(index, 4), 2)


def products(steering, values, first, rows):
    real = steering[rows, pl.ds(first, HALF)].T.astype(jnp.float32)
    imag = steering[rows, pl.ds(CHANNELS + first, HALF)].T.astype(jnp.float32)
    total = dot(parts((real - imag) * values), steering[rows, :CHANNELS], 0)
    return total + dot(parts((real + imag) * values), steering[rows, CHANNELS:], 0)


def cross_half(spectra, placed, half, out):
    count = spectra.shape[0]
    first = pl.multiple_of(half * HALF, HALF)
    row = pl.multiple_of(lax.axis_index("band") * count, count)
    cross_real, cross_imag = spectra[:, :CHANNELS], spectra[:, CHANNELS:]
    placed[...] = jnp.zeros_like(placed)
    placed[pl.ds(row, count), :] = (cross_real + cross_imag) * 0.5
    out[...] = placed[:, pl.ds(first, HALF)].T

    @pl.when(lax.div(row, HALF) == half)
    def _():
        here = pl.ds(pl.multiple_of(row - first, count), count)
        out[here, :] = out[here, :] + (cross_real - cross_imag) * 0.5


def first_kernel(steering_far, estimates_far, spectra_far, out, steering, estimates, spectra, placed, sems):
    points = steering_far.shape[0]
    whole = steering.at[pl.ds(0, points)]
    loads = [
        pltpu.make_async_copy(estimates_far, estimates, sems.at[0]),
        pltpu.make_async_copy(spectra_far, spectra, sems.at[1]),
        pltpu.make_async_copy(steering_far, whole, sems.at[2]),
    ]
    for load in loads:
        load.start()
    half = 1 - place(lax.axis_index("band"))
    loads[1].wait()
    cross_half(spectra, placed, half, out)
    loads[0].wait()
    values = estimates[...].astype(jnp.float32)
    line = lax.broadcasted_iota(jnp.int32, (TAIL, 2 * CHANNELS), 0)
    rest = jnp.zeros((1, 4 * CHANNELS - points), jnp.float32)
    back = jnp.concatenate([values[:, 2 * CHANNELS :], rest], axis=1)
    tail = jnp.where(line == 0, values[:, : 2 * CHANNELS], jnp.where(line == 1, back, 0.0))
    steering[pl.ds(points, TAIL), :] = tail.astype(steering.dtype)
    loads[2].wait()
    own = products(steering, values, pl.multiple_of(half * HALF, HALF), slice(0, points))
    out[...] = out[...] - folded(own)


def second_kernel(steering, estimates, spectra, out, placed):
    half = place(lax.axis_index("band"))
    values = estimates[...].astype(jnp.float32)
    own = products(steering, values, pl.multiple_of(half * HALF, HALF), slice(0, estimates.shape[1]))
    cross_half(spectra, placed, half, out)
    out[...] = out[...] - folded(own)


def ready_kernel(steering, twin_steering, *outs):
    for rows, (minus, plus, power) in ((steering, outs[:3]), (twin_steering, outs[3:])):
        points = minus.shape[1]
        real = rows[:points, :CHANNELS].T.astype(jnp.float32)
        imag = rows[:points, CHANNELS:].T.astype(jnp.float32)
        minus[...] = real - imag
        plus[...] = real + imag
        power[...] = jnp.sum(real * real + imag * imag, axis=0, keepdims=True)


def form(total, half, steering, minus, plus, here):
    pieces = parts(total)
    rows = pl.ds(pl.multiple_of(half * HALF, HALF), HALF)
    terms = folded(dot(pieces, steering[here, :CHANNELS], 1)) * minus[rows, here]
    terms = terms + folded(dot(pieces, steering[here, CHANNELS:], 1)) * plus[rows, here]
    return jnp.sum(terms, axis=0, keepdims=True)


def near_kernel(mine, *refs):
    partial = refs[-1]
    half = place(lax.axis_index("band"))
    for side, (steering, minus, plus) in enumerate((refs[:3], refs[3:6])):
        for s in range(0, minus.shape[1], CHUNK):
            here = slice(s, s + CHUNK)
            partial[side : side + 1, here] = form(mine[...], half, steering, minus, plus, here)


def far_kernel(other, partial, *refs):
    updated = refs[-1]
    updated[...] = jnp.zeros_like(updated)
    half = 1 - place(lax.axis_index("band"))
    scale = 1.0 / (CHANNELS * CHANNELS)
    for side, (steering, minus, plus, power) in enumerate((refs[:4], refs[4:8])):
        points = minus.shape[1]
        tail = steering[points:, :].astype(jnp.float32)
        estimates = jnp.concatenate([tail[:1], tail[1:2, : points - 2 * CHANNELS]], axis=1)
        for s in range(0, points, CHUNK):
            here = slice(s, s + CHUNK)
            whole = partial[side : side + 1, here] + form(other[...], half, steering, minus, plus, here)
            diag = power[:, here] * power[:, here] * scale
            result = jnp.maximum(estimates[:, here] + whole * scale / diag, 0.0)
            for t in range(0, CHUNK, LANES):
                line = side * SUBLANES + (s + t) // LANES
                updated[line : line + 1, :] = result[:, t : t + LANES]


def partner(index, step):
    z, y, core = index // 4, index // 2 % 2, index % 2
    kind = ORDER[(z + y + core) % 2][step]
    z, y = (z, 1 - y) if kind == 0 else (z ^ kind, y)
    return (z * 2 + y) * 2 + 1 - core


def across(value, bit):
    flip = int(bit in FLIPPED)
    pairs = [(b * 8 + k, (b ^ flip) * 8 + (k ^ bit)) for b in range(16) for k in range(8)]
    moved = lax.ppermute(value, ("band", "blk"), pairs)
    if flip:
        moved = jnp.concatenate([moved[SUBLANES:], moved[:SUBLANES]], axis=0)
    return value + moved


def body(steering, estimates, spectra):
    points = steering.shape[1]
    steering, spectra = steering[0], spectra[0]
    scratch = [pltpu.VMEM((CHANNELS, CHANNELS), jnp.float32)]
    operands = tuple(pltpu.with_memory_space_constraint(a, pltpu.HBM) for a in (steering, estimates, spectra))
    send, steering, estimates, spectra = call(
        first_kernel,
        (
            wide(HALF, CHANNELS),
            jax.ShapeDtypeStruct((points + TAIL, 2 * CHANNELS), steering.dtype),
            jax.ShapeDtypeStruct(estimates.shape, estimates.dtype),
            wide(*spectra.shape),
        ),
        operands,
        scratch + [pltpu.SemaphoreType.DMA((3,))],
        spec=ANY,
    )
    keep = call(second_kernel, wide(HALF, CHANNELS), (steering, estimates, spectra), scratch)
    twins = [(i, i ^ 1) for i in range(16)]
    total = keep + lax.ppermute(send, "band", twins)
    later, total = lax.optimization_barrier((steering, total))
    twin_steering = lax.ppermute(later, "band", twins)
    flat = wide(CHANNELS, points)
    shapes = (flat, flat, wide(1, points))
    for step in range(3):
        total = total + lax.ppermute(total, "band", [(i, partner(i, step)) for i in range(16)])
        if step == 0:
            total, twin_steering = lax.optimization_barrier((total, twin_steering))
            ready = call(ready_kernel, shapes * 2, (steering, twin_steering))
        if step == 1:
            total, ready = lax.optimization_barrier((total, ready))
    other = lax.ppermute(total, "band", twins)
    partial = call(
        near_kernel, wide(2, points), (total, steering, *ready[:2], twin_steering, *ready[3:5])
    )
    lines = points // LANES
    both = call(
        far_kernel,
        wide(2 * SUBLANES, LANES),
        (other, partial, steering, *ready[:3], twin_steering, *ready[3:]),
    )
    updated = both[:lines].reshape(1, points)
    summed = both
    for bit in (1, 2, 6):
        summed = across(summed, bit)
    return updated, summed[:lines].reshape(points)


def solution(mesh):
    return jax.shard_map(
        body,
        mesh=mesh,
        in_specs=(P("blk", "band", None), P("blk", "band"), P("blk", "band", None)),
        out_specs=(P("blk", "band"), P("band")),
        check_vma=False,
    )
```

```python
import functools

import jax
import jax.numpy as jnp
from jax import lax
from jax.experimental import pallas as pl
from jax.experimental.pallas import tpu as pltpu
from jax.sharding import PartitionSpec as P

CHANNELS = 256
HALF = CHANNELS // 2
CHUNK = 256
FIRST = 768
LANES = 128
TAIL = 16
FLIPPED = (1, 2)
SUBLANES = 8
ORDER = ((0, 3, 1), (3, 1, 0))
VMEM = pl.BlockSpec(memory_space=pltpu.VMEM)
ANY = pl.BlockSpec(memory_space=pl.ANY)


def wide(*shape):
    return jax.ShapeDtypeStruct(shape, jnp.float32)


def call(kernel, out_shape, operands, scratch=(), flops=1 << 28, spec=VMEM, room=24):
    return pl.pallas_call(
        kernel,
        out_shape=out_shape,
        in_specs=[spec] * len(operands),
        out_specs=jax.tree.map(lambda _: VMEM, out_shape),
        scratch_shapes=list(scratch),
        compiler_params=pltpu.CompilerParams(vmem_limit_bytes=room << 20),
        cost_estimate=pl.CostEstimate(flops=flops, bytes_accessed=1 << 20, transcendentals=0),
    )(*operands)


def parts(value):
    high = value.astype(jnp.bfloat16)
    low = (value - high.astype(jnp.float32)).astype(jnp.bfloat16)
    return jnp.concatenate([high, low], axis=0)


def dot(left, right, contract):
    dims = (((1,), (contract,)), ((), ()))
    return lax.dot_general(left, right, dims, preferred_element_type=jnp.float32)


def folded(both):
    rows = both.shape[0] // 2
    return both[:rows] + both[rows:]


def place(index):
    return lax.rem(index + lax.div(index, 2) + lax.div(index, 4), 2)


def products(steering, values, first, rows):
    real = steering[rows, pl.ds(first, HALF)].T.astype(jnp.float32)
    imag = steering[rows, pl.ds(CHANNELS + first, HALF)].T.astype(jnp.float32)
    total = dot(parts((real - imag) * values), steering[rows, :CHANNELS], 0)
    return total + dot(parts((real + imag) * values), steering[rows, CHANNELS:], 0)


def cross_half(spectra, placed, half, out):
    count = spectra.shape[0]
    first = pl.multiple_of(half * HALF, HALF)
    row = pl.multiple_of(lax.axis_index("band") * count, count)
    cross_real, cross_imag = spectra[:, :CHANNELS], spectra[:, CHANNELS:]
    placed[...] = jnp.zeros_like(placed)
    placed[pl.ds(row, count), :] = (cross_real + cross_imag) * 0.5
    out[...] = placed[:, pl.ds(first, HALF)].T

    @pl.when(lax.div(row, HALF) == half)
    def _():
        here = pl.ds(pl.multiple_of(row - first, count), count)
        out[here, :] = out[here, :] + (cross_real - cross_imag) * 0.5


def first_kernel(steering_far, estimates_far, spectra_far, out, steering, estimates, spectra, placed, sems):
    points = steering_far.shape[0]
    whole = steering.at[pl.ds(0, points)]
    loads = [
        pltpu.make_async_copy(estimates_far, estimates, sems.at[0]),
        pltpu.make_async_copy(spectra_far, spectra, sems.at[1]),
        pltpu.make_async_copy(steering_far, whole, sems.at[2]),
    ]
    for load in loads:
        load.start()
    half = 1 - place(lax.axis_index("band"))
    loads[1].wait()
    cross_half(spectra, placed, half, out)
    loads[0].wait()
    values = estimates[...].astype(jnp.float32)
    line = lax.broadcasted_iota(jnp.int32, (TAIL, 2 * CHANNELS), 0)
    rest = jnp.zeros((1, 4 * CHANNELS - points), jnp.float32)
    back = jnp.concatenate([values[:, 2 * CHANNELS :], rest], axis=1)
    tail = jnp.where(line == 0, values[:, : 2 * CHANNELS], jnp.where(line == 1, back, 0.0))
    steering[pl.ds(points, TAIL), :] = tail.astype(steering.dtype)
    loads[2].wait()
    own = products(steering, values, pl.multiple_of(half * HALF, HALF), slice(0, points))
    out[...] = out[...] - folded(own)


def second_kernel(steering, estimates, spectra, out, placed):
    half = place(lax.axis_index("band"))
    values = estimates[...].astype(jnp.float32)
    own = products(steering, values, pl.multiple_of(half * HALF, HALF), slice(0, estimates.shape[1]))
    cross_half(spectra, placed, half, out)
    out[...] = out[...] - folded(own)


def ready_kernel(steering, twin_steering, minus, plus, twin_minus, twin_plus, values, diag):
    scale = 1.0 / (CHANNELS * CHANNELS)
    values[...] = jnp.zeros_like(values)
    diag[...] = jnp.ones_like(diag)
    sides = ((steering, minus, plus), (twin_steering, twin_minus, twin_plus))
    for side, (rows, less, more) in enumerate(sides):
        points = less.shape[1]
        real = rows[:points, :CHANNELS].T.astype(jnp.float32)
        imag = rows[:points, CHANNELS:].T.astype(jnp.float32)
        less[...] = real - imag
        more[...] = real + imag
        power = jnp.sum(real * real + imag * imag, axis=0, keepdims=True)
        tail = rows[points:, :].astype(jnp.float32)
        estimates = jnp.concatenate([tail[:1], tail[1:2, : points - 2 * CHANNELS]], axis=1)
        for t in range(0, points, LANES):
            line = side * SUBLANES + t // LANES
            values[line : line + 1, :] = estimates[:, t : t + LANES]
            diag[line : line + 1, :] = power[:, t : t + LANES] * power[:, t : t + LANES] * scale


def form_kernel(mine, steering, minus, plus, twin_steering, twin_minus, twin_plus, partial):
    half = place(lax.axis_index("band"))
    pieces = parts(mine[...])
    rows = pl.ds(pl.multiple_of(half * HALF, HALF), HALF)
    partial[...] = jnp.zeros_like(partial)
    sides = ((steering, minus, plus), (twin_steering, twin_minus, twin_plus))
    for side, (points, less, more) in enumerate(sides):
        for s in range(0, less.shape[1], CHUNK):
            here = slice(s, s + CHUNK)
            terms = folded(dot(pieces, points[here, :CHANNELS], 1)) * less[rows, here]
            terms = terms + folded(dot(pieces, points[here, CHANNELS:], 1)) * more[rows, here]
            sums = jnp.sum(terms, axis=0, keepdims=True)
            for t in range(0, CHUNK, LANES):
                line = side * SUBLANES + (s + t) // LANES
                partial[line : line + 1, :] = sums[:, t : t + LANES]


def partner(index, step):
    z, y, core = index // 4, index // 2 % 2, index % 2
    kind = ORDER[(z + y + core) % 2][step]
    z, y = (z, 1 - y) if kind == 0 else (z ^ kind, y)
    return (z * 2 + y) * 2 + 1 - core


def swapped(value):
    return jnp.concatenate([value[SUBLANES:], value[:SUBLANES]], axis=0)


def across(value, bit):
    flip = int(bit in FLIPPED)
    pairs = [(b * 8 + k, (b ^ flip) * 8 + (k ^ bit)) for b in range(16) for k in range(8)]
    moved = lax.ppermute(value, ("band", "blk"), pairs)
    return value + (swapped(moved) if flip else moved)


def body(steering, estimates, spectra):
    points = steering.shape[1]
    steering, spectra = steering[0], spectra[0]
    scratch = [pltpu.VMEM((CHANNELS, CHANNELS), jnp.float32)]
    operands = tuple(pltpu.with_memory_space_constraint(a, pltpu.HBM) for a in (steering, estimates, spectra))
    send, steering, estimates, spectra = call(
        first_kernel,
        (
            wide(HALF, CHANNELS),
            jax.ShapeDtypeStruct((points + TAIL, 2 * CHANNELS), steering.dtype),
            jax.ShapeDtypeStruct(estimates.shape, estimates.dtype),
            wide(*spectra.shape),
        ),
        operands,
        scratch + [pltpu.SemaphoreType.DMA((3,))],
        spec=ANY,
    )
    keep = call(second_kernel, wide(HALF, CHANNELS), (steering, estimates, spectra), scratch)
    twins = [(i, i ^ 1) for i in range(16)]
    total = keep + lax.ppermute(send, "band", twins)
    later, total = lax.optimization_barrier((steering, total))
    twin_steering = lax.ppermute(later, "band", twins)
    flat = wide(CHANNELS, points)
    lined = wide(2 * SUBLANES, LANES)
    for step in range(3):
        total = total + lax.ppermute(total, "band", [(i, partner(i, step)) for i in range(16)])
        if step == 0:
            total, twin_steering = lax.optimization_barrier((total, twin_steering))
            ready = call(ready_kernel, (flat,) * 4 + (lined,) * 2, (steering, twin_steering))
        if step == 1:
            total, ready = lax.optimization_barrier((total, ready))
    minus, plus, twin_minus, twin_plus, values, diag = ready
    partial = call(form_kernel, lined, (total, steering, minus, plus, twin_steering, twin_minus, twin_plus))
    forms = partial + swapped(lax.ppermute(partial, "band", twins))
    both = jnp.maximum(values + forms * (1.0 / (CHANNELS * CHANNELS)) / diag, 0.0)
    lines = points // LANES
    updated = both[:lines].reshape(1, points)
    summed = both
    for bit in (1, 2, 6):
        summed = across(summed, bit)
    return updated, summed[:lines].reshape(points)


def solution(mesh):
    return jax.shard_map(
        body,
        mesh=mesh,
        in_specs=(P("blk", "band", None), P("blk", "band"), P("blk", "band", None)),
        out_specs=(P("blk", "band"), P("band")),
        check_vma=False,
    )
```

```python
import functools

import jax
import jax.numpy as jnp
from jax import lax
from jax.experimental import pallas as pl
from jax.experimental.pallas import tpu as pltpu
from jax.sharding import PartitionSpec as P

CHANNELS = 256
HALF = CHANNELS // 2
CHUNK = 256
FIRST = 768
LANES = 128
FLIPPED = (1, 2)
SUBLANES = 8
ORDER = ((0, 3, 1), (3, 1, 0))
VMEM = pl.BlockSpec(memory_space=pltpu.VMEM)
ANY = pl.BlockSpec(memory_space=pl.ANY)


def wide(*shape):
    return jax.ShapeDtypeStruct(shape, jnp.float32)


def call(kernel, out_shape, operands, scratch=(), flops=1 << 28, spec=VMEM, room=24):
    return pl.pallas_call(
        kernel,
        out_shape=out_shape,
        in_specs=[spec] * len(operands),
        out_specs=jax.tree.map(lambda _: VMEM, out_shape),
        scratch_shapes=list(scratch),
        compiler_params=pltpu.CompilerParams(vmem_limit_bytes=room << 20),
        cost_estimate=pl.CostEstimate(flops=flops, bytes_accessed=1 << 20, transcendentals=0),
    )(*operands)


def parts(value):
    high = value.astype(jnp.bfloat16)
    low = (value - high.astype(jnp.float32)).astype(jnp.bfloat16)
    return jnp.concatenate([high, low], axis=0)


def dot(left, right, contract):
    dims = (((1,), (contract,)), ((), ()))
    return lax.dot_general(left, right, dims, preferred_element_type=jnp.float32)


def folded(both):
    rows = both.shape[0] // 2
    return both[:rows] + both[rows:]


def place(index):
    return lax.rem(index + lax.div(index, 4), 2)


def products(steering, values, first, rows):
    real = steering[rows, pl.ds(first, HALF)].T.astype(jnp.float32)
    imag = steering[rows, pl.ds(CHANNELS + first, HALF)].T.astype(jnp.float32)
    total = dot(parts((real - imag) * values), steering[rows, :CHANNELS], 0)
    return total + dot(parts((real + imag) * values), steering[rows, CHANNELS:], 0)


def cross_half(spectra, index, placed, half, out):
    count = spectra.shape[0]
    first = pl.multiple_of(half * HALF, HALF)
    row = pl.multiple_of(index * count, count)
    cross_real, cross_imag = spectra[:, :CHANNELS], spectra[:, CHANNELS:]
    placed[...] = jnp.zeros_like(placed)
    placed[pl.ds(row, count), :] = (cross_real + cross_imag) * 0.5
    out[...] = out[...] + placed[:, pl.ds(first, HALF)].T

    @pl.when(lax.div(row, HALF) == half)
    def _():
        here = pl.ds(pl.multiple_of(row - first, count), count)
        out[here, :] = out[here, :] + (cross_real - cross_imag) * 0.5


def own_kernel(steering_far, estimates_far, spectra_far, out, steering, estimates, placed, spectra, sems):
    loads = [
        pltpu.make_async_copy(estimates_far, estimates, sems.at[0]),
        pltpu.make_async_copy(spectra_far, spectra, sems.at[1]),
        pltpu.make_async_copy(steering_far, steering, sems.at[2]),
    ]
    for load in loads:
        load.start()
    index = lax.axis_index("band")
    half = place(index)
    out[...] = jnp.zeros_like(out)
    loads[1].wait()
    cross_half(spectra, index, placed, half, out)
    loads[0].wait()
    values = estimates[...].astype(jnp.float32)
    loads[2].wait()
    own = products(steering, values, pl.multiple_of(half * HALF, HALF), slice(None))
    out[...] = out[...] - folded(own)


def twin_kernel(own, steering, estimates, spectra, out, placed):
    index = lax.axis_index("band")
    half = place(index)
    out[...] = own[...]
    cross_half(spectra, index + 1 - 2 * lax.rem(index, 2), placed, half, out)
    values = estimates[...].astype(jnp.float32)
    more = products(steering, values, pl.multiple_of(half * HALF, HALF), slice(None))
    out[...] = out[...] - folded(more)


def ready_kernel(steering, estimates, twin_steering, twin_estimates, minus, plus, twin_minus, twin_plus, values, diag):
    scale = 1.0 / (CHANNELS * CHANNELS)
    values[...] = jnp.zeros_like(values)
    diag[...] = jnp.ones_like(diag)
    sides = ((steering, estimates, minus, plus), (twin_steering, twin_estimates, twin_minus, twin_plus))
    for side, (rows, levels, less, more) in enumerate(sides):
        points = less.shape[1]
        real = rows[:, :CHANNELS].T.astype(jnp.float32)
        imag = rows[:, CHANNELS:].T.astype(jnp.float32)
        less[...] = real - imag
        more[...] = real + imag
        power = jnp.sum(real * real + imag * imag, axis=0, keepdims=True)
        level = levels[...].astype(jnp.float32)
        for t in range(0, points, LANES):
            line = side * SUBLANES + t // LANES
            values[line : line + 1, :] = level[:, t : t + LANES]
            diag[line : line + 1, :] = power[:, t : t + LANES] * power[:, t : t + LANES] * scale


def form_kernel(mine, steering, minus, plus, twin_steering, twin_minus, twin_plus, partial):
    half = place(lax.axis_index("band"))
    pieces = parts(mine[...])
    rows = pl.ds(pl.multiple_of(half * HALF, HALF), HALF)
    partial[...] = jnp.zeros_like(partial)
    sides = ((steering, minus, plus), (twin_steering, twin_minus, twin_plus))
    for side, (points, less, more) in enumerate(sides):
        for s in range(0, less.shape[1], CHUNK):
            here = slice(s, s + CHUNK)
            terms = folded(dot(pieces, points[here, :CHANNELS], 1)) * less[rows, here]
            terms = terms + folded(dot(pieces, points[here, CHANNELS:], 1)) * more[rows, here]
            sums = jnp.sum(terms, axis=0, keepdims=True)
            for t in range(0, CHUNK, LANES):
                line = side * SUBLANES + (s + t) // LANES
                partial[line : line + 1, :] = sums[:, t : t + LANES]


def partner(index, step):
    z, y, core = index // 4, index // 2 % 2, index % 2
    kind = ORDER[(z + core) % 2][step]
    z, y = (z, 1 - y) if kind == 0 else (z ^ kind, y)
    return (z * 2 + y) * 2 + (core if kind == 0 else 1 - core)


def swapped(value):
    return jnp.concatenate([value[SUBLANES:], value[:SUBLANES]], axis=0)


def across(value, bit):
    flip = int(bit in FLIPPED)
    pairs = [(b * 8 + k, (b ^ flip) * 8 + (k ^ bit)) for b in range(16) for k in range(8)]
    moved = lax.ppermute(value, ("band", "blk"), pairs)
    return value + (swapped(moved) if flip else moved)


def body(steering, estimates, spectra):
    points = steering.shape[1]
    steering, spectra = steering[0], spectra[0]
    scratch = [pltpu.VMEM((CHANNELS, CHANNELS), jnp.float32)]
    operands = tuple(pltpu.with_memory_space_constraint(a, pltpu.HBM) for a in (steering, estimates, spectra))
    twins = [(i, i ^ 1) for i in range(16)]
    twin_steering, twin_estimates, twin_spectra = (
        pltpu.with_memory_space_constraint(lax.ppermute(a, "band", twins), pltpu.VMEM) for a in operands
    )
    own, steering, estimates = call(
        own_kernel,
        (wide(HALF, CHANNELS), *(jax.ShapeDtypeStruct(a.shape, a.dtype) for a in (steering, estimates))),
        operands,
        scratch + [pltpu.VMEM(spectra.shape, jnp.float32), pltpu.SemaphoreType.DMA((3,))],
        spec=ANY,
    )
    twin_operands = (twin_steering, twin_estimates, twin_spectra)
    total = call(twin_kernel, wide(HALF, CHANNELS), (own, *twin_operands), scratch)
    flat = wide(CHANNELS, points)
    lined = wide(2 * SUBLANES, LANES)
    for step in range(3):
        total = total + lax.ppermute(total, "band", [(i, partner(i, step)) for i in range(16)])
        if step == 0:
            total, later = lax.optimization_barrier((total, twin_steering))
            ready = call(ready_kernel, (flat,) * 4 + (lined,) * 2, (steering, estimates, later, twin_estimates))
        if step == 1:
            total, ready = lax.optimization_barrier((total, ready))
    minus, plus, twin_minus, twin_plus, values, diag = ready
    partial = call(form_kernel, lined, (total, steering, minus, plus, twin_steering, twin_minus, twin_plus))
    forms = partial + swapped(lax.ppermute(partial, "band", twins))
    both = jnp.maximum(values + forms * (1.0 / (CHANNELS * CHANNELS)) / diag, 0.0)
    lines = points // LANES
    updated = both[:lines].reshape(1, points)
    summed = both
    for bit in (1, 2, 6):
        summed = across(summed, bit)
    return updated, summed[:lines].reshape(points)


def solution(mesh):
    return jax.shard_map(
        body,
        mesh=mesh,
        in_specs=(P("blk", "band", None), P("blk", "band"), P("blk", "band", None)),
        out_specs=(P("blk", "band"), P("band")),
        check_vma=False,
    )
```

```python
import functools

import jax
import jax.numpy as jnp
from jax import lax
from jax.experimental import pallas as pl
from jax.experimental.pallas import tpu as pltpu
from jax.sharding import PartitionSpec as P

CHANNELS = 256
HALF = CHANNELS // 2
CHUNK = 256
FIRST = 768
LANES = 128
FLIPPED = (1, 6)
SUBLANES = 8
ORDER = ((0, 3, 1), (3, 1, 0))
VMEM = pl.BlockSpec(memory_space=pltpu.VMEM)
ANY = pl.BlockSpec(memory_space=pl.ANY)


def wide(*shape):
    return jax.ShapeDtypeStruct(shape, jnp.float32)


def call(kernel, out_shape, operands, scratch=(), flops=1 << 28, spec=VMEM, room=24):
    return pl.pallas_call(
        kernel,
        out_shape=out_shape,
        in_specs=[spec] * len(operands),
        out_specs=jax.tree.map(lambda _: VMEM, out_shape),
        scratch_shapes=list(scratch),
        compiler_params=pltpu.CompilerParams(vmem_limit_bytes=room << 20),
        cost_estimate=pl.CostEstimate(flops=flops, bytes_accessed=1 << 20, transcendentals=0),
    )(*operands)


def parts(value):
    high = value.astype(jnp.bfloat16)
    low = (value - high.astype(jnp.float32)).astype(jnp.bfloat16)
    return jnp.concatenate([high, low], axis=0)


def dot(left, right, contract):
    dims = (((1,), (contract,)), ((), ()))
    return lax.dot_general(left, right, dims, preferred_element_type=jnp.float32)


def folded(both):
    rows = both.shape[0] // 2
    return both[:rows] + both[rows:]


def place(index):
    return lax.rem(index + lax.div(index, 4), 2)


def products(steering, values, first, rows):
    real = steering[rows, pl.ds(first, HALF)].T.astype(jnp.float32)
    imag = steering[rows, pl.ds(CHANNELS + first, HALF)].T.astype(jnp.float32)
    total = dot(parts((real - imag) * values), steering[rows, :CHANNELS], 0)
    return total + dot(parts((real + imag) * values), steering[rows, CHANNELS:], 0)


def cross_half(spectra, index, placed, half, out):
    count = spectra.shape[0]
    first = pl.multiple_of(half * HALF, HALF)
    row = pl.multiple_of(index * count, count)
    cross_real, cross_imag = spectra[:, :CHANNELS], spectra[:, CHANNELS:]
    placed[...] = jnp.zeros_like(placed)
    placed[pl.ds(row, count), :] = (cross_real + cross_imag) * 0.5
    out[...] = out[...] + placed[:, pl.ds(first, HALF)].T

    @pl.when(lax.div(row, HALF) == half)
    def _():
        here = pl.ds(pl.multiple_of(row - first, count), count)
        out[here, :] = out[here, :] + (cross_real - cross_imag) * 0.5


def own_kernel(steering_far, estimates_far, spectra_far, out, steering, estimates, placed, spectra, sems):
    loads = [
        pltpu.make_async_copy(estimates_far, estimates, sems.at[0]),
        pltpu.make_async_copy(spectra_far, spectra, sems.at[1]),
        pltpu.make_async_copy(steering_far, steering, sems.at[2]),
    ]
    for load in loads:
        load.start()
    index = lax.axis_index("band")
    half = place(index)
    out[...] = jnp.zeros_like(out)
    loads[1].wait()
    cross_half(spectra, index, placed, half, out)
    loads[0].wait()
    values = estimates[...].astype(jnp.float32)
    loads[2].wait()
    own = products(steering, values, pl.multiple_of(half * HALF, HALF), slice(None))
    out[...] = out[...] - folded(own)


def twin_kernel(own, steering, estimates, spectra, out, placed):
    index = lax.axis_index("band")
    half = place(index)
    out[...] = own[...]
    cross_half(spectra, index + 1 - 2 * lax.rem(index, 2), placed, half, out)
    values = estimates[...].astype(jnp.float32)
    more = products(steering, values, pl.multiple_of(half * HALF, HALF), slice(None))
    out[...] = out[...] - folded(more)


def ready_kernel(steering, estimates, twin_steering, twin_estimates, minus, plus, twin_minus, twin_plus, values, diag):
    scale = 1.0 / (CHANNELS * CHANNELS)
    values[...] = jnp.zeros_like(values)
    diag[...] = jnp.ones_like(diag)
    sides = ((steering, estimates, minus, plus), (twin_steering, twin_estimates, twin_minus, twin_plus))
    for side, (rows, levels, less, more) in enumerate(sides):
        points = less.shape[1]
        real = rows[:, :CHANNELS].T.astype(jnp.float32)
        imag = rows[:, CHANNELS:].T.astype(jnp.float32)
        less[...] = real - imag
        more[...] = real + imag
        power = jnp.sum(real * real + imag * imag, axis=0, keepdims=True)
        level = levels[...].astype(jnp.float32)
        for t in range(0, points, LANES):
            line = side * SUBLANES + t // LANES
            values[line : line + 1, :] = level[:, t : t + LANES]
            diag[line : line + 1, :] = power[:, t : t + LANES] * power[:, t : t + LANES] * scale


def form_kernel(mine, steering, minus, plus, twin_steering, twin_minus, twin_plus, partial):
    half = place(lax.axis_index("band"))
    pieces = parts(mine[...])
    rows = pl.ds(pl.multiple_of(half * HALF, HALF), HALF)
    partial[...] = jnp.zeros_like(partial)
    sides = ((steering, minus, plus), (twin_steering, twin_minus, twin_plus))
    for side, (points, less, more) in enumerate(sides):
        for s in range(0, less.shape[1], CHUNK):
            here = slice(s, s + CHUNK)
            terms = folded(dot(pieces, points[here, :CHANNELS], 1)) * less[rows, here]
            terms = terms + folded(dot(pieces, points[here, CHANNELS:], 1)) * more[rows, here]
            sums = jnp.sum(terms, axis=0, keepdims=True)
            for t in range(0, CHUNK, LANES):
                line = side * SUBLANES + (s + t) // LANES
                partial[line : line + 1, :] = sums[:, t : t + LANES]


def partner(index, step):
    z, y, core = index // 4, index // 2 % 2, index % 2
    kind = ORDER[(z + core) % 2][step]
    z, y = (z, 1 - y) if kind == 0 else (z ^ kind, y)
    return (z * 2 + y) * 2 + (core if kind == 0 else 1 - core)


def swapped(value):
    return jnp.concatenate([value[SUBLANES:], value[:SUBLANES]], axis=0)


def across(value, bit):
    flip = int(bit in FLIPPED)
    pairs = [(b * 8 + k, (b ^ flip) * 8 + (k ^ bit)) for b in range(16) for k in range(8)]
    moved = lax.ppermute(value, ("band", "blk"), pairs)
    return value + (swapped(moved) if flip else moved)


def body(steering, estimates, spectra):
    points = steering.shape[1]
    steering, spectra = steering[0], spectra[0]
    scratch = [pltpu.VMEM((CHANNELS, CHANNELS), jnp.float32)]
    operands = tuple(pltpu.with_memory_space_constraint(a, pltpu.HBM) for a in (steering, estimates, spectra))
    twins = [(i, i ^ 1) for i in range(16)]
    twin_steering, twin_estimates, twin_spectra = (
        pltpu.with_memory_space_constraint(lax.ppermute(a, "band", twins), pltpu.VMEM) for a in operands
    )
    own, steering, estimates = call(
        own_kernel,
        (wide(HALF, CHANNELS), *(jax.ShapeDtypeStruct(a.shape, a.dtype) for a in (steering, estimates))),
        operands,
        scratch + [pltpu.VMEM(spectra.shape, jnp.float32), pltpu.SemaphoreType.DMA((3,))],
        spec=ANY,
    )
    twin_operands = (twin_steering, twin_estimates, twin_spectra)
    total = call(twin_kernel, wide(HALF, CHANNELS), (own, *twin_operands), scratch)
    flat = wide(CHANNELS, points)
    lined = wide(2 * SUBLANES, LANES)
    for step in range(3):
        total = total + lax.ppermute(total, "band", [(i, partner(i, step)) for i in range(16)])
        if step == 0:
            total, later = lax.optimization_barrier((total, twin_steering))
            ready = call(ready_kernel, (flat,) * 4 + (lined,) * 2, (steering, estimates, later, twin_estimates))
        if step == 1:
            total, ready = lax.optimization_barrier((total, ready))
    minus, plus, twin_minus, twin_plus, values, diag = ready
    partial = call(form_kernel, lined, (total, steering, minus, plus, twin_steering, twin_minus, twin_plus))
    forms = partial + swapped(lax.ppermute(partial, "band", twins))
    both = jnp.maximum(values + forms * (1.0 / (CHANNELS * CHANNELS)) / diag, 0.0)
    lines = points // LANES
    updated = both[:lines].reshape(1, points)
    summed = both
    for bit in (6, 1, 2):
        summed = across(summed, bit)
    return updated, summed[:lines].reshape(points)


def solution(mesh):
    return jax.shard_map(
        body,
        mesh=mesh,
        in_specs=(P("blk", "band", None), P("blk", "band"), P("blk", "band", None)),
        out_specs=(P("blk", "band"), P("band")),
        check_vma=False,
    )
```

```python
import functools

import jax
import jax.numpy as jnp
from jax import lax
from jax.experimental import pallas as pl
from jax.experimental.pallas import tpu as pltpu
from jax.sharding import PartitionSpec as P

CHANNELS = 256
HALF = CHANNELS // 2
CHUNK = 256
FIRST = 768
LANES = 128
FLIPPED = (1, 6)
SUBLANES = 8
ORDER = ((0, 3, 1), (3, 1, 0))
VMEM = pl.BlockSpec(memory_space=pltpu.VMEM)
ANY = pl.BlockSpec(memory_space=pl.ANY)


def wide(*shape):
    return jax.ShapeDtypeStruct(shape, jnp.float32)


def call(kernel, out_shape, operands, scratch=(), flops=1 << 28, spec=VMEM, room=24):
    return pl.pallas_call(
        kernel,
        out_shape=out_shape,
        in_specs=[spec] * len(operands),
        out_specs=jax.tree.map(lambda _: VMEM, out_shape),
        scratch_shapes=list(scratch),
        compiler_params=pltpu.CompilerParams(vmem_limit_bytes=room << 20),
        cost_estimate=pl.CostEstimate(flops=flops, bytes_accessed=1 << 20, transcendentals=0),
    )(*operands)


def parts(value):
    high = value.astype(jnp.bfloat16)
    low = (value - high.astype(jnp.float32)).astype(jnp.bfloat16)
    return jnp.concatenate([high, low], axis=0)


def dot(left, right, contract):
    dims = (((1,), (contract,)), ((), ()))
    return lax.dot_general(left, right, dims, preferred_element_type=jnp.float32)


def folded(both):
    rows = both.shape[0] // 2
    return both[:rows] + both[rows:]


def place(index):
    return lax.rem(index + lax.div(index, 4), 2)


def products(steering, values, first, rows):
    real = steering[rows, pl.ds(first, HALF)].T.astype(jnp.float32)
    imag = steering[rows, pl.ds(CHANNELS + first, HALF)].T.astype(jnp.float32)
    total = dot(parts((real - imag) * values), steering[rows, :CHANNELS], 0)
    return total + dot(parts((real + imag) * values), steering[rows, CHANNELS:], 0)


def cross_half(spectra, index, placed, half, out):
    count = spectra.shape[0]
    first = pl.multiple_of(half * HALF, HALF)
    row = pl.multiple_of(index * count, count)
    cross_real, cross_imag = spectra[:, :CHANNELS], spectra[:, CHANNELS:]
    placed[...] = jnp.zeros_like(placed)
    placed[pl.ds(row, count), :] = (cross_real + cross_imag) * 0.5
    out[...] = out[...] + placed[:, pl.ds(first, HALF)].T

    @pl.when(lax.div(row, HALF) == half)
    def _():
        here = pl.ds(pl.multiple_of(row - first, count), count)
        out[here, :] = out[here, :] + (cross_real - cross_imag) * 0.5


def own_kernel(steering_far, estimates_far, spectra_far, out, steering, estimates, placed, spectra, sems):
    loads = [
        pltpu.make_async_copy(estimates_far, estimates, sems.at[0]),
        pltpu.make_async_copy(spectra_far, spectra, sems.at[1]),
        pltpu.make_async_copy(steering_far, steering, sems.at[2]),
    ]
    for load in reversed(loads):
        load.start()
    index = lax.axis_index("band")
    half = place(index)
    out[...] = jnp.zeros_like(out)
    loads[1].wait()
    cross_half(spectra, index, placed, half, out)
    loads[0].wait()
    values = estimates[...].astype(jnp.float32)
    loads[2].wait()
    own = products(steering, values, pl.multiple_of(half * HALF, HALF), slice(None))
    out[...] = out[...] - folded(own)


def twin_kernel(own, steering, estimates, spectra, out, placed):
    index = lax.axis_index("band")
    half = place(index)
    out[...] = own[...]
    cross_half(spectra, index + 1 - 2 * lax.rem(index, 2), placed, half, out)
    values = estimates[...].astype(jnp.float32)
    more = products(steering, values, pl.multiple_of(half * HALF, HALF), slice(None))
    out[...] = out[...] - folded(more)


def ready_kernel(steering, estimates, twin_steering, twin_estimates, minus, plus, twin_minus, twin_plus, values, diag):
    scale = 1.0 / (CHANNELS * CHANNELS)
    values[...] = jnp.zeros_like(values)
    diag[...] = jnp.ones_like(diag)
    sides = ((steering, estimates, minus, plus), (twin_steering, twin_estimates, twin_minus, twin_plus))
    for side, (rows, levels, less, more) in enumerate(sides):
        points = less.shape[1]
        real = rows[:, :CHANNELS].T.astype(jnp.float32)
        imag = rows[:, CHANNELS:].T.astype(jnp.float32)
        less[...] = real - imag
        more[...] = real + imag
        power = jnp.sum(real * real + imag * imag, axis=0, keepdims=True)
        level = levels[...].astype(jnp.float32)
        for t in range(0, points, LANES):
            line = side * SUBLANES + t // LANES
            values[line : line + 1, :] = level[:, t : t + LANES]
            diag[line : line + 1, :] = power[:, t : t + LANES] * power[:, t : t + LANES] * scale


def form_kernel(mine, steering, minus, plus, twin_steering, twin_minus, twin_plus, partial):
    half = place(lax.axis_index("band"))
    pieces = parts(mine[...])
    rows = pl.ds(pl.multiple_of(half * HALF, HALF), HALF)
    partial[...] = jnp.zeros_like(partial)
    sides = ((steering, minus, plus), (twin_steering, twin_minus, twin_plus))
    for side, (points, less, more) in enumerate(sides):
        for s in range(0, less.shape[1], CHUNK):
            here = slice(s, s + CHUNK)
            terms = folded(dot(pieces, points[here, :CHANNELS], 1)) * less[rows, here]
            terms = terms + folded(dot(pieces, points[here, CHANNELS:], 1)) * more[rows, here]
            sums = jnp.sum(terms, axis=0, keepdims=True)
            for t in range(0, CHUNK, LANES):
                line = side * SUBLANES + (s + t) // LANES
                partial[line : line + 1, :] = sums[:, t : t + LANES]


def partner(index, step):
    z, y, core = index // 4, index // 2 % 2, index % 2
    kind = ORDER[(z + core) % 2][step]
    z, y = (z, 1 - y) if kind == 0 else (z ^ kind, y)
    return (z * 2 + y) * 2 + (core if kind == 0 else 1 - core)


def swapped(value):
    return jnp.concatenate([value[SUBLANES:], value[:SUBLANES]], axis=0)


def across(value, bit):
    flip = int(bit in FLIPPED)
    pairs = [(b * 8 + k, (b ^ flip) * 8 + (k ^ bit)) for b in range(16) for k in range(8)]
    moved = lax.ppermute(value, ("band", "blk"), pairs)
    return value + (swapped(moved) if flip else moved)


def body(steering, estimates, spectra):
    points = steering.shape[1]
    steering, spectra = steering[0], spectra[0]
    scratch = [pltpu.VMEM((CHANNELS, CHANNELS), jnp.float32)]
    operands = tuple(pltpu.with_memory_space_constraint(a, pltpu.HBM) for a in (steering, estimates, spectra))
    twins = [(i, i ^ 1) for i in range(16)]
    twin_steering, twin_estimates, twin_spectra = (
        pltpu.with_memory_space_constraint(lax.ppermute(a, "band", twins), pltpu.VMEM) for a in operands
    )
    own, steering, estimates = call(
        own_kernel,
        (wide(HALF, CHANNELS), *(jax.ShapeDtypeStruct(a.shape, a.dtype) for a in (steering, estimates))),
        operands,
        scratch + [pltpu.VMEM(spectra.shape, jnp.float32), pltpu.SemaphoreType.DMA((3,))],
        spec=ANY,
    )
    twin_operands = (twin_steering, twin_estimates, twin_spectra)
    total = call(twin_kernel, wide(HALF, CHANNELS), (own, *twin_operands), scratch)
    flat = wide(CHANNELS, points)
    lined = wide(2 * SUBLANES, LANES)
    for step in range(3):
        total = total + lax.ppermute(total, "band", [(i, partner(i, step)) for i in range(16)])
        if step == 0:
            total, later = lax.optimization_barrier((total, twin_steering))
            ready = call(ready_kernel, (flat,) * 4 + (lined,) * 2, (steering, estimates, later, twin_estimates))
        if step == 1:
            total, ready = lax.optimization_barrier((total, ready))
    minus, plus, twin_minus, twin_plus, values, diag = ready
    partial = call(form_kernel, lined, (total, steering, minus, plus, twin_steering, twin_minus, twin_plus))
    forms = partial + swapped(lax.ppermute(partial, "band", twins))
    both = jnp.maximum(values + forms * (1.0 / (CHANNELS * CHANNELS)) / diag, 0.0)
    lines = points // LANES
    updated = both[:lines].reshape(1, points)
    summed = both
    for bit in (6, 1, 2):
        summed = across(summed, bit)
    return updated, summed[:lines].reshape(points)


def solution(mesh):
    return jax.shard_map(
        body,
        mesh=mesh,
        in_specs=(P("blk", "band", None), P("blk", "band"), P("blk", "band", None)),
        out_specs=(P("blk", "band"), P("band")),
        check_vma=False,
    )
```
